256 devices in a mesh: replica: 4 (over x), fsdp: 32 (over y_hi, z, core), tensor: 2 (over y_lo).
Axes of the slice: x: 4, y: 4 (y_hi: 2, y_lo: 2; y = y_hi * 2 + y_lo), z: 8, core: 2. Of those that a mesh axis runs over, the one named last changes fastest.
Arguments:
- tokens: bfloat16 [4, 16384, 8192], P('replica', 'fsdp'), may hold values from -6 to 6
- pseudo_grad: bfloat16 [4, 8192, 1024], P('replica', 'fsdp', 'tensor'), may hold values from -0.078125 to 0.078125
- anchor: float32 [8192, 2, 4, 128], P('fsdp', 'tensor', 'replica'), may hold values from -0.0625 to 0.0625
- momentum: float32 [8192, 2, 4, 128], P('fsdp', 'tensor', 'replica'), may hold values from -0.0625 to 0.0625
Outputs:
- keys: bfloat16 [4, 16384, 1024], P('replica', 'fsdp', 'tensor')
- anchor_new: float32 [8192, 2, 4, 128], P('fsdp', 'tensor', 'replica')
- momentum_new: float32 [8192, 2, 4, 128], P('fsdp', 'tensor', 'replica')
The draws below stay inside these ranges and needn't reach their ends.
All inputs are finite; a program needn't handle non-finite values.
Results may differ from the reference program's by a relative error of at most 0.015.
Values may be sent and summed in bfloat16 or wider, within the bound.
No kernel may reach another device: no remote copies, remote signals or barrier semaphores. Data moves between devices by JAX's collectives and lax.ppermute only.
A program may use at most 64 MiB of HBM per device.

```python
import jax
import jax.numpy as jnp
from jax import lax

D = 8192
KVD = 1024
CW = 128
TOKENS = 16384
N_REPLICA = 4
N_TENSOR = 2


def with_spikes(values, rng, source, target, blocks, factor):
    owner, partner = [(jnp.arange(values.shape[position]) // (values.shape[position] // blocks)).reshape([-1 if axis == position else 1 for axis in range(values.ndim)]) for position in (source, target)]
    chosen = jax.random.permutation(rng, blocks)[partner]
    strong = (owner == chosen) | (owner == (partner + blocks // 2) % blocks)
    return jnp.where(strong, factor * values, values)


def steps_of(rng, extent, pieces, smallest, top_value):
    loudness = 1.0
    for dim, shards_of in pieces:
        draws = jax.random.uniform(jax.random.fold_in(jax.random.fold_in(rng, 6), dim), (shards_of,), jnp.float32, smallest / len(pieces), top_value / len(pieces))
        loudness = loudness * jnp.repeat(jnp.exp(draws), extent[dim] // shards_of).reshape((-1,) + (1,) * (len(extent) - 1 - dim))
    return loudness


def scatter_about(rng, extent, spread, limit, split=(), held_as=jnp.bfloat16):
    drawn = jax.random.normal(rng, extent, jnp.float32) * spread
    if len(split) > 0:
        drawn = steps_of(rng, extent, split, -0.22, 0.18) * drawn
    return jnp.clip(drawn, min=-limit, max=limit).astype(held_as)


def bell_draw_with(key, extent, scale, limit, shards, heavy, dtype=jnp.bfloat16):
    drawn = scale * jax.random.normal(key, extent, jnp.float32)
    if shards:
        drawn = drawn * steps_of(key, extent, shards, -0.22, 0.18)
    return jnp.clip(with_spikes(drawn, jax.random.fold_in(key, 3), *heavy), -limit, limit).astype(dtype)


def setup_inputs(seed: int = 0) -> dict:
    splits = jax.random.split(jax.random.key(seed), 5)
    return {
        "tokens": scatter_about(splits[0], (N_REPLICA, TOKENS, D), 1.0, 6.0, ((0, 4), (1, 32))),
        "pseudo_grad": bell_draw_with(splits[1], (N_REPLICA, D, KVD), 0.01, 0.078125, ((0, 4), (1, 32), (2, 2)), (0, 2, 4, 2.0)),
        "anchor": scatter_about(splits[2], (D, N_TENSOR, N_REPLICA, CW), D ** -0.5, 0.0625, ((0, 32), (1, 2), (2, 4)), jnp.float32),
        "momentum": scatter_about(splits[3], (D, N_TENSOR, N_REPLICA, CW), 0.01, 0.0625, ((0, 32), (1, 2), (2, 4)), jnp.float32),
    }


outer_rate = 0.7
momentum_keep = 0.9


def reference(tokens, pseudo_grad, anchor, momentum):
    summed = jnp.sum(pseudo_grad.astype(jnp.float32), axis=0)
    delta = (summed * (1.0 / N_REPLICA)).reshape(anchor.shape)
    momentum_new = momentum_keep * momentum + delta
    anchor_new = anchor - outer_rate * (delta + momentum_keep * momentum_new)
    weights = anchor_new.astype(jnp.bfloat16).reshape(D, KVD)

    def project(island_tokens):
        return jnp.dot(island_tokens, weights, preferred_element_type=jnp.float32).astype(jnp.bfloat16)

    keys = lax.map(project, tokens)
    return keys, anchor_new, momentum_new
```

```python
import functools

import jax
import jax.numpy as jnp
from jax import lax
from jax.experimental import pallas as pl
from jax.experimental.pallas import tpu as pltpu
from jax.sharding import PartitionSpec as P

outer_rate = 0.7
momentum_keep = 0.9

AXES = ("replica", "fsdp", "tensor")
STEPS = (1, -1, 2)
VMEM_LIMIT = 48 * 1024 * 1024


def pairs(move):
    out = []
    for x in range(4):
        for y in range(2):
            for z in range(8):
                for c in range(2):
                    for t in range(2):
                        to_x, to_y, to_z, to_c = move(x, y, z, c)
                        source = (x * 32 + y * 16 + z * 2 + c) * 2 + t
                        target = ((to_x % 4) * 32 + (to_y % 2) * 16 + (to_z % 8) * 2 + to_c % 2) * 2 + t
                        out.append((source, target))
    return out


def send(value, move):
    return lax.ppermute(value, AXES, pairs(move))


def along_x(step):
    return lambda x, y, z, c: (x + step, y, z, c)


def early(step):
    return lambda x, y, z, c: (x + step, y, z, c) if c == 0 else (x, y, z + step, c)


def late(step):
    return lambda x, y, z, c: (x, y, z + step, c) if c == 0 else (x + step, y, z, c)


def position():
    index = lax.axis_index("fsdp")
    return lax.axis_index("replica"), index // 16, (index // 2) % 8, index % 2


def wrap(value):
    return lax.rem(value + 4, 4)


def call(kernel, out_shape, *, flops=0, size=1, scratch=(), in_specs=None):
    specs = {} if in_specs is None else {"in_specs": in_specs}
    return pl.pallas_call(
        kernel,
        out_shape=out_shape,
        **specs,
        scratch_shapes=list(scratch),
        compiler_params=pltpu.CompilerParams(vmem_limit_bytes=VMEM_LIMIT),
        cost_estimate=pl.CostEstimate(flops=flops, bytes_accessed=size, transcendentals=0),
    )


def split_kernel(grad, *outs):
    x, _, _, _ = position()
    for step, out in zip((0,) + STEPS, outs):
        first = pl.multiple_of(wrap(x + step) * 128, 128)
        out[...] = grad[:, pl.ds(first, 128)]


def update_kernel(own, one, two, three, anchor, momentum, anchor_new, momentum_new, weights):
    total = own[...].astype(jnp.float32) + one[...].astype(jnp.float32)
    total = total + (two[...].astype(jnp.float32) + three[...].astype(jnp.float32))
    delta = total * 0.25
    kept = momentum_keep * momentum[...] + delta
    moved = anchor[...] - outer_rate * (delta + momentum_keep * kept)
    momentum_new[...] = kept
    anchor_new[...] = moved
    weights[...] = moved.astype(jnp.bfloat16)


def join_pairs_kernel(own, by_y, by_z, by_both, out):
    _, y, z, _ = position()
    here = y * 2 + z // 4
    other_y, other_z = 1 - y, 1 - z // 4
    out[here] = own[...]
    out[other_y * 2 + z // 4] = by_y[...]
    out[y * 2 + other_z] = by_z[...]
    out[other_y * 2 + other_z] = by_both[...]


def join_four_kernel(own, one, two, three, out):
    x, _, z, c = position()
    here = jnp.where(c == 0, x, z % 4)
    for step, piece in zip((0,) + STEPS, (own, one, two, three)):
        out[pl.ds(wrap(here - step) * 4, 4)] = piece[...]


def pack_kernel(own, other, out, sems):
    _, _, _, c = position()
    copies = []
    for side, tokens in enumerate((own, other)):
        for near in range(4):
            for pair in range(4):
                row = (pair // 2) * 16 + ((pair % 2) * 4 + near) * 2
                source = pl.multiple_of((row + c) * 256, 256)
                copies.append(
                    pltpu.make_async_copy(
                        tokens.at[:, pl.ds(source, 256)],
                        out.at[pl.ds(side * 512, 512), pl.ds((near * 4 + pair) * 256, 256)],
                        sems.at[len(copies)],
                    )
                )
    for copy in copies:
        copy.start()
    for copy in copies:
        copy.wait()


def product_kernel(steps, first_row, rows, has_start, packed, left, right, *rest):
    start, out = (rest[0], rest[1]) if has_start else (None, rest[0])
    x, _, z, c = position()
    tile = 256

    @pl.when(c == 0)
    def _():
        @pl.loop(0, rows // tile)
        def _(m):
            here = pl.ds(pl.multiple_of(m * tile, tile), tile)
            there = pl.ds(pl.multiple_of(first_row + m * tile, tile), tile)
            for half in range(2):
                columns = pl.ds(half * 256, 256)
                total = start[here, columns] if has_start else None
                for step, piece in zip(steps, (left, right)):
                    near = pl.multiple_of(wrap(z % 4 - step) * 1024, 1024)
                    block = jnp.concatenate(
                        [piece[pl.ds((half * 2 + q) * 4, 4)].reshape(1024, 128) for q in range(2)], axis=1
                    )
                    term = jnp.dot(packed[there, pl.ds(near, 1024)], block, preferred_element_type=jnp.float32)
                    total = term if total is None else total + term
                out[here, columns] = total

    @pl.when(c == 1)
    def _():
        @pl.loop(0, rows // tile)
        def _(m):
            here = pl.ds(pl.multiple_of(m * tile, tile), tile)
            there = pl.ds(pl.multiple_of(first_row + m * tile, tile), tile)
            block = jnp.concatenate([left[...].reshape(4096, 128), right[...].reshape(4096, 128)], axis=1)
            term = jnp.dot(packed[there, :], block, preferred_element_type=jnp.float32)
            if has_start:
                out[here, :] = start[here, :]
            for k, step in enumerate(steps):
                column = pl.multiple_of(wrap(x - step) * 128, 128)
                out[here, pl.ds(column, 128)] = term[:, k * 128 : (k + 1) * 128]


def product(packed, left, right, steps, first_row, rows, start=None):
    args = (packed, left, right) + (() if start is None else (start,))
    return call(
        functools.partial(product_kernel, steps, first_row, rows, start is not None),
        jax.ShapeDtypeStruct((rows, 512), jnp.float32),
        flops=2 * rows * 2048 * 512,
        size=rows * 8192 + 2 * 2**20,
    )(*args)


def per_device(tokens, pseudo_grad, anchor, momentum):
    block = jax.ShapeDtypeStruct((256, 128), jnp.bfloat16)
    state = jax.ShapeDtypeStruct((256, 128), jnp.float32)
    own_tokens = tokens[0]
    grads = call(split_kernel, (block,) * 4, size=2**19)(pseudo_grad[0])
    arrived = [send(grads[k + 1], along_x(step)) for k, step in enumerate(STEPS)]
    other_tokens = send(own_tokens, lambda x, y, z, c: (x, y, z, c + 1))
    anchor_new, momentum_new, weights = call(update_kernel, (state, state, block), size=2**20)(
        grads[0], *arrived, anchor.reshape(256, 128), momentum.reshape(256, 128)
    )
    swaps = [
        send(weights, lambda x, y, z, c: (x, y + 1, z, c)),
        send(weights, lambda x, y, z, c: (x, y, z + 4, c)),
        send(weights, lambda x, y, z, c: (x, y + 1, z + 4, c)),
    ]
    four = call(join_pairs_kernel, jax.ShapeDtypeStruct((4, 256, 128), jnp.bfloat16), size=2**19)(weights, *swaps)
    fours = [send(four, early(step)) for step in STEPS]
    mine = call(join_four_kernel, jax.ShapeDtypeStruct((16, 256, 128), jnp.bfloat16), size=2**21)(four, *fours)
    packed = call(
        pack_kernel,
        jax.ShapeDtypeStruct((1024, 4096), jnp.bfloat16),
        size=2**24,
        scratch=(pltpu.SemaphoreType.DMA((32,)),),
        in_specs=[pl.BlockSpec(memory_space=pl.ANY)] * 2,
    )(own_tokens, other_tokens)
    far = {step: send(mine, late(step)) for step in STEPS}
    first = product(packed, mine, far[1], (0, 1), 0, 1024)
    away = product(packed, far[-1], far[2], (-1, 2), 512, 512, first[512:])
    returned = send(away.astype(jnp.bfloat16), lambda x, y, z, c: (x, y, z, c + 1))
    here = product(packed, far[-1], far[2], (-1, 2), 0, 512, first[:512])
    keys = (here + returned.astype(jnp.float32)).astype(jnp.bfloat16)[None]
    return keys, anchor_new.reshape(anchor.shape), momentum_new.reshape(momentum.shape)


def solution(mesh):
    return jax.shard_map(
        per_device,
        mesh=mesh,
        in_specs=(
            P("replica", "fsdp", None),
            P("replica", "fsdp", "tensor"),
            P("fsdp", "tensor", "replica", None),
            P("fsdp", "tensor", "replica", None),
        ),
        out_specs=(
            P("replica", "fsdp", "tensor"),
            P("fsdp", "tensor", "replica", None),
            P("fsdp", "tensor", "replica", None),
        ),
        check_vma=False,
    )
```

```python
import functools

import jax
import jax.numpy as jnp
from jax import lax
from jax.experimental import pallas as pl
from jax.experimental.pallas import tpu as pltpu
from jax.sharding import PartitionSpec as P

outer_rate = 0.7
momentum_keep = 0.9

AXES = ("replica", "fsdp", "tensor")
STEPS = (1, -1, 2)
VMEM_LIMIT = 20 * 1024 * 1024


def pairs(move):
    out = []
    for x in range(4):
        for y in range(2):
            for z in range(8):
                for c in range(2):
                    for t in range(2):
                        to_x, to_y, to_z, to_c = move(x, y, z, c)
                        source = (x * 32 + y * 16 + z * 2 + c) * 2 + t
                        target = ((to_x % 4) * 32 + (to_y % 2) * 16 + (to_z % 8) * 2 + to_c % 2) * 2 + t
                        out.append((source, target))
    return out


def send(value, move):
    return lax.ppermute(value, AXES, pairs(move))


def along_x(step):
    return lambda x, y, z, c: (x + step, y, z, c)


def early(step):
    def move(x, y, z, c):
        along_z = step if step != 2 or z % 2 == 0 else -step
        return (x + step, y, z, c) if c == 0 else (x, y, z + along_z, c)

    return move


def late(step):
    return lambda x, y, z, c: (x, y, z + step, c) if c == 0 else (x + step, y, z, c)


def position():
    index = lax.axis_index("fsdp")
    return lax.axis_index("replica"), index // 16, (index // 2) % 8, index % 2


def wrap(value):
    return lax.rem(value + 4, 4)


def call(kernel, out_shape, *, flops=0, size=1, scratch=(), in_specs=None):
    specs = {} if in_specs is None else {"in_specs": in_specs}
    return pl.pallas_call(
        kernel,
        out_shape=out_shape,
        **specs,
        scratch_shapes=list(scratch),
        compiler_params=pltpu.CompilerParams(vmem_limit_bytes=VMEM_LIMIT),
        cost_estimate=pl.CostEstimate(flops=flops, bytes_accessed=size, transcendentals=0),
    )


def split_kernel(grad, *outs):
    x, _, _, _ = position()
    for step, out in zip((0,) + STEPS, outs):
        first = pl.multiple_of(wrap(x + step) * 128, 128)
        out[...] = grad[:, pl.ds(first, 128)]


def prepare_kernel(anchor, momentum, anchor_out, kept_out):
    anchor_out[...] = anchor[...]
    kept_out[...] = momentum_keep * momentum[...]


def step_of(own, one, two, three, anchor, kept):
    total = own[...].astype(jnp.float32) + one[...].astype(jnp.float32)
    total = total + (two[...].astype(jnp.float32) + three[...].astype(jnp.float32))
    delta = total * 0.25
    momentum_new = kept[...] + delta
    return anchor[...] - outer_rate * (delta + momentum_keep * momentum_new), momentum_new


def weights_kernel(own, one, two, three, anchor, kept, weights):
    weights[...] = step_of(own, one, two, three, anchor, kept)[0].astype(jnp.bfloat16)


def state_kernel(own, one, two, three, anchor, kept, anchor_new, momentum_new):
    anchor_new[...], momentum_new[...] = step_of(own, one, two, three, anchor, kept)


def join_y_kernel(own, other, out):
    _, y, _, _ = position()
    out[y] = own[...]
    out[1 - y] = other[...]


def join_far_kernel(own, other, out):
    _, _, z, _ = position()
    far = z // 4
    out[pl.ds(far * 2, 2)] = own[...]
    out[pl.ds((1 - far) * 2, 2)] = other[...]


def join_four_kernel(own, one, two, three, low, high):
    x, _, z, c = position()
    here = jnp.where(c == 0, x, z % 4)
    for step, piece in zip((0,) + STEPS, (own, one, two, three)):
        place = wrap(here - step)
        row = lax.rem(place, 2) * 4

        @pl.when(place < 2)
        def _():
            low[pl.ds(row, 4)] = piece[...]

        @pl.when(place >= 2)
        def _():
            high[pl.ds(row, 4)] = piece[...]


def pack_kernel(own, other, out, sems):
    _, _, _, c = position()
    copies = []
    for side, tokens in enumerate((own, other)):
        for near in range(4):
            for pair in range(4):
                row = (pair % 2) * 16 + ((pair // 2) * 4 + near) * 2
                source = pl.multiple_of((row + c) * 256, 256)
                copies.append(
                    pltpu.make_async_copy(
                        tokens.at[:, pl.ds(source, 256)],
                        out.at[pl.ds(side * 512, 512), pl.ds((near * 4 + pair) * 256, 256)],
                        sems.at[len(copies)],
                    )
                )
    for copy in copies:
        copy.start()
    for copy in copies:
        copy.wait()


def product_kernel(steps, sides, has_start, packed, *refs):
    count = len(steps)
    lows, highs = refs[:count], refs[count : 2 * count]
    starts = refs[2 * count : 2 * count + len(sides)] if has_start else (None,) * len(sides)
    outs = refs[len(refs) - len(sides) :]
    x, _, z, c = position()

    @pl.when(c == 0)
    def _():
        for side, start, out in zip(sides, starts, outs):
            rows = pl.ds(side * 512, 512)
            for half, pieces in enumerate((lows, highs)):
                columns = pl.ds(half * 256, 256)
                total = start[:, columns] if has_start else None
                for step, piece in zip(steps, pieces):
                    near = pl.multiple_of(wrap(z % 4 - step) * 1024, 1024)
                    block = jnp.concatenate([piece[pl.ds(q * 4, 4)].reshape(1024, 128) for q in range(2)], axis=1)
                    term = jnp.dot(packed[rows, pl.ds(near, 1024)], block, preferred_element_type=jnp.float32)
                    total = term if total is None else total + term
                out[:, columns] = total.astype(out.dtype)

    @pl.when(c == 1)
    def _():
        for side, start, out in zip(sides, starts, outs):
            rows = pl.ds(side * 512, 512)
            total = None
            for half, pieces in enumerate((lows, highs)):
                block = jnp.concatenate([piece[...].reshape(2048, 128) for piece in pieces], axis=1)
                term = jnp.dot(packed[rows, pl.ds(half * 2048, 2048)], block, preferred_element_type=jnp.float32)
                total = term if total is None else total + term
            if has_start:
                out[...] = start[...].astype(out.dtype)
            for k, step in enumerate(steps):
                column = pl.multiple_of(wrap(x - step) * 128, 128)
                out[:, pl.ds(column, 128)] = total[:, k * 128 : (k + 1) * 128].astype(out.dtype)


def product(packed, steps, lows, highs, sides, starts=(), dtype=jnp.float32):
    count = len(steps) * len(sides)
    return call(
        functools.partial(product_kernel, steps, sides, bool(starts)),
        (jax.ShapeDtypeStruct((512, 512), dtype),) * len(sides),
        flops=2 * count * 512 * 1024 * 512,
        size=count * 2**20,
    )(packed, *lows, *highs, *starts)


def per_device(tokens, pseudo_grad, anchor, momentum):
    def blocks(count):
        return jax.ShapeDtypeStruct((count, 256, 128), jnp.bfloat16)

    block = jax.ShapeDtypeStruct((256, 128), jnp.bfloat16)
    state = jax.ShapeDtypeStruct((256, 128), jnp.float32)
    own_tokens = tokens[0]
    grads = call(split_kernel, (block,) * 4, size=2**19)(pseudo_grad[0])
    arrived = [send(grads[k + 1], along_x(step)) for k, step in enumerate(STEPS)]
    other_tokens = send(own_tokens, lambda x, y, z, c: (x, y, z, c + 1))
    prepared = call(prepare_kernel, (state, state), size=2**19)(anchor.reshape(256, 128), momentum.reshape(256, 128))
    (weights,) = call(weights_kernel, (block,), size=2**19)(grads[0], *arrived, *prepared)
    anchor_new, momentum_new = call(state_kernel, (state, state), size=2**20)(grads[0], *arrived, *prepared)
    by_y = send(weights, lambda x, y, z, c: (x, y + 1, z, c))
    (two,) = call(join_y_kernel, (blocks(2),), size=2**18)(weights, by_y)
    by_far = send(two, lambda x, y, z, c: (x, y, z + 4, c))
    (four,) = call(join_far_kernel, (blocks(4),), size=2**19)(two, by_far)
    fours = [send(four, early(step)) for step in STEPS]
    low, high = call(join_four_kernel, (blocks(8), blocks(8)), size=2**21)(four, *fours)
    (packed,) = call(
        pack_kernel,
        (jax.ShapeDtypeStruct((1024, 4096), jnp.bfloat16),),
        size=2**24,
        scratch=(pltpu.SemaphoreType.DMA((32,)),),
        in_specs=[pl.BlockSpec(memory_space=pl.ANY), pl.BlockSpec(memory_space=pltpu.VMEM)],
    )(own_tokens, other_tokens)
    low_up, high_down = send(low, late(1)), send(high, late(-1))
    high_up, low_down = send(high, late(1)), send(low, late(-1))
    low_two, high_two = send(low_up, late(1)), send(high_down, late(-1))
    starts = product(packed, (0,), (low,), (high,), (0, 1))
    starts = product(packed, (1, -1), (low_up, low_down), (high_up, high_down), (0, 1), starts)
    (away,) = product(packed, (2,), (low_two,), (high_two,), (1,), starts[1:], jnp.bfloat16)
    returned = send(away, lambda x, y, z, c: (x, y, z, c + 1))
    (here,) = product(packed, (2,), (low_two,), (high_two,), (0,), starts[:1])
    keys = (here + returned.astype(jnp.float32)).astype(jnp.bfloat16)[None]
    return keys, anchor_new.reshape(anchor.shape), momentum_new.reshape(momentum.shape)


def solution(mesh):
    return jax.shard_map(
        per_device,
        mesh=mesh,
        in_specs=(
            P("replica", "fsdp", None),
            P("replica", "fsdp", "tensor"),
            P("fsdp", "tensor", "replica", None),
            P("fsdp", "tensor", "replica", None),
        ),
        out_specs=(
            P("replica", "fsdp", "tensor"),
            P("fsdp", "tensor", "replica", None),
            P("fsdp", "tensor", "replica", None),
        ),
        check_vma=False,
    )
```

```python
import functools

import jax
import jax.numpy as jnp
from jax import lax
from jax.experimental import pallas as pl
from jax.experimental.pallas import tpu as pltpu
from jax.sharding import PartitionSpec as P

outer_rate = 0.7
momentum_keep = 0.9

AXES = ("replica", "fsdp", "tensor")
STEPS = (1, -1, 2)
VMEM_LIMIT = 20 * 1024 * 1024


def pairs(move):
    out = []
    for x in range(4):
        for y in range(2):
            for z in range(8):
                for c in range(2):
                    for t in range(2):
                        to_x, to_y, to_z, to_c = move(x, y, z, c)
                        source = (x * 32 + y * 16 + z * 2 + c) * 2 + t
                        target = ((to_x % 4) * 32 + (to_y % 2) * 16 + (to_z % 8) * 2 + to_c % 2) * 2 + t
                        out.append((source, target))
    return out


def send(value, move):
    return lax.ppermute(value, AXES, pairs(move))


def along_x(step):
    return lambda x, y, z, c: (x + step, y, z, c)


def early(step):
    def move(x, y, z, c):
        along_z = step if step != 2 or z % 2 == 0 else -step
        return (x + step, y, z, c) if c == 0 else (x, y, z + along_z, c)

    return move


def late(step):
    return lambda x, y, z, c: (x, y, z + step, c) if c == 0 else (x + step, y, z, c)


def position():
    index = lax.axis_index("fsdp")
    return lax.axis_index("replica"), index // 16, (index // 2) % 8, index % 2


def wrap(value):
    return lax.rem(value + 4, 4)


def call(kernel, out_shape, *, flops=0, size=1, scratch=(), in_specs=None, limit=VMEM_LIMIT):
    specs = {} if in_specs is None else {"in_specs": in_specs}
    return pl.pallas_call(
        kernel,
        out_shape=out_shape,
        **specs,
        scratch_shapes=list(scratch),
        compiler_params=pltpu.CompilerParams(vmem_limit_bytes=limit),
        cost_estimate=pl.CostEstimate(flops=flops, bytes_accessed=size, transcendentals=0),
    )


def split_kernel(grad, *outs):
    x, _, _, _ = position()
    for step, out in zip((0,) + STEPS, outs):
        first = pl.multiple_of(wrap(x + step) * 128, 128)
        out[...] = grad[:, pl.ds(first, 128)]


def prepare_kernel(anchor, momentum, anchor_out, kept_out):
    anchor_out[...] = anchor[...]
    kept_out[...] = momentum_keep * momentum[...]


def step_of(own, one, two, three, anchor, kept):
    total = own[...].astype(jnp.float32) + one[...].astype(jnp.float32)
    total = total + (two[...].astype(jnp.float32) + three[...].astype(jnp.float32))
    delta = total * 0.25
    momentum_new = kept[...] + delta
    return anchor[...] - outer_rate * (delta + momentum_keep * momentum_new), momentum_new


def weights_kernel(own, one, two, three, anchor, kept, weights):
    weights[...] = step_of(own, one, two, three, anchor, kept)[0].astype(jnp.bfloat16)


def state_kernel(own, one, two, three, anchor, kept, anchor_new, momentum_new):
    anchor_new[...], momentum_new[...] = step_of(own, one, two, three, anchor, kept)


def join_y_kernel(own, other, out):
    _, y, _, _ = position()
    out[y] = own[...]
    out[1 - y] = other[...]


def join_far_kernel(own, other, out):
    _, _, z, _ = position()
    far = z // 4
    out[pl.ds(far * 2, 2)] = own[...]
    out[pl.ds((1 - far) * 2, 2)] = other[...]


def join_four_kernel(own, one, two, three, low, high):
    x, _, z, c = position()
    here = jnp.where(c == 0, x, z % 4)
    for step, piece in zip((0,) + STEPS, (own, one, two, three)):
        place = wrap(here - step)
        row = lax.rem(place, 2) * 4

        @pl.when(place < 2)
        def _():
            low[pl.ds(row, 4)] = piece[...]

        @pl.when(place >= 2)
        def _():
            high[pl.ds(row, 4)] = piece[...]


def pack_kernel(tokens, out, sems):
    _, _, _, c = position()
    copies = []
    for near in range(4):
        for pair in range(4):
            row = (pair % 2) * 16 + ((pair // 2) * 4 + near) * 2
            source = pl.multiple_of((row + c) * 256, 256)
            copies.append(
                pltpu.make_async_copy(
                    tokens.at[:, pl.ds(source, 256)],
                    out.at[:, pl.ds((near * 4 + pair) * 256, 256)],
                    sems.at[len(copies)],
                )
            )
    for copy in copies:
        copy.start()
    for copy in copies:
        copy.wait()


def pack(tokens, space, limit):
    return call(
        pack_kernel,
        jax.ShapeDtypeStruct((512, 4096), jnp.bfloat16),
        size=2**23,
        scratch=(pltpu.SemaphoreType.DMA((16,)),),
        in_specs=[pl.BlockSpec(memory_space=space)],
        limit=limit,
    )(tokens)


def product_kernel(steps, sides, has_start, *refs):
    packed, refs = refs[: len(sides)], refs[len(sides) :]
    count = len(steps)
    lows, highs = refs[:count], refs[count : 2 * count]
    starts = refs[2 * count : 2 * count + len(sides)] if has_start else (None,) * len(sides)
    outs = refs[len(refs) - len(sides) :]
    x, _, z, c = position()

    @pl.when(c == 0)
    def _():
        for rows, start, out in zip(packed, starts, outs):
            for half, pieces in enumerate((lows, highs)):
                columns = pl.ds(half * 256, 256)
                total = start[:, columns] if has_start else None
                for step, piece in zip(steps, pieces):
                    near = pl.multiple_of(wrap(z % 4 - step) * 1024, 1024)
                    block = jnp.concatenate([piece[pl.ds(q * 4, 4)].reshape(1024, 128) for q in range(2)], axis=1)
                    term = jnp.dot(rows[:, pl.ds(near, 1024)], block, preferred_element_type=jnp.float32)
                    total = term if total is None else total + term
                out[:, columns] = total.astype(out.dtype)

    @pl.when(c == 1)
    def _():
        for rows, start, out in zip(packed, starts, outs):
            total = None
            for half, pieces in enumerate((lows, highs)):
                block = jnp.concatenate([piece[...].reshape(2048, 128) for piece in pieces], axis=1)
                term = jnp.dot(rows[:, pl.ds(half * 2048, 2048)], block, preferred_element_type=jnp.float32)
                total = term if total is None else total + term
            if has_start:
                out[...] = start[...].astype(out.dtype)
            for k, step in enumerate(steps):
                column = pl.multiple_of(wrap(x - step) * 128, 128)
                out[:, pl.ds(column, 128)] = total[:, k * 128 : (k + 1) * 128].astype(out.dtype)


def product(packed, steps, lows, highs, sides, starts=(), dtype=jnp.float32):
    count = len(steps) * len(sides)
    return call(
        functools.partial(product_kernel, steps, sides, bool(starts)),
        (jax.ShapeDtypeStruct((512, 512), dtype),) * len(sides),
        flops=2 * count * 512 * 1024 * 512,
        size=count * 2**20,
    )(*[packed[side] for side in sides], *lows, *highs, *starts)


def per_device(tokens, pseudo_grad, anchor, momentum):
    def blocks(count):
        return jax.ShapeDtypeStruct((count, 256, 128), jnp.bfloat16)

    block = jax.ShapeDtypeStruct((256, 128), jnp.bfloat16)
    state = jax.ShapeDtypeStruct((256, 128), jnp.float32)
    own_tokens = tokens[0]
    grads = call(split_kernel, (block,) * 4, size=2**19)(pseudo_grad[0])
    arrived = [send(grads[k + 1], along_x(step)) for k, step in enumerate(STEPS)]
    other_tokens = send(own_tokens, lambda x, y, z, c: (x, y, z, c + 1))
    prepared = call(prepare_kernel, (state, state), size=2**19)(anchor.reshape(256, 128), momentum.reshape(256, 128))
    (weights,) = call(weights_kernel, (block,), size=2**19)(grads[0], *arrived, *prepared)
    anchor_new, momentum_new = call(state_kernel, (state, state), size=2**20)(grads[0], *arrived, *prepared)
    by_y = send(weights, lambda x, y, z, c: (x, y + 1, z, c))
    (two,) = call(join_y_kernel, (blocks(2),), size=2**18)(weights, by_y)
    by_far = send(two, lambda x, y, z, c: (x, y, z + 4, c))
    packed_own = pack(own_tokens, pltpu.HBM, 44 * 1024 * 1024)
    two, packed_own = lax.optimization_barrier((two, packed_own))
    (four,) = call(join_far_kernel, (blocks(4),), size=2**19)(two, by_far)
    fours = [send(four, early(step)) for step in STEPS]
    packed_other = pack(other_tokens, pltpu.VMEM, VMEM_LIMIT)
    four, packed_other = lax.optimization_barrier((four, packed_other))
    packed = (packed_own, packed_other)
    low, high = call(join_four_kernel, (blocks(8), blocks(8)), size=2**21)(four, *fours)
    low_up, high_down = send(low, late(1)), send(high, late(-1))
    high_up, low_down = send(high, late(1)), send(low, late(-1))
    starts = product(packed, (0,), (low,), (high,), (0, 1))
    low_up, high_down, *starts = lax.optimization_barrier((low_up, high_down, *starts))
    low_two, high_two = send(low_up, late(1)), send(high_down, late(-1))
    starts = product(packed, (1, -1), (low_up, low_down), (high_up, high_down), (0, 1), starts)
    (away,) = product(packed, (2,), (low_two,), (high_two,), (1,), starts[1:], jnp.bfloat16)
    returned = send(away, lambda x, y, z, c: (x, y, z, c + 1))
    (here,) = product(packed, (2,), (low_two,), (high_two,), (0,), starts[:1])
    keys = (here + returned.astype(jnp.float32)).astype(jnp.bfloat16)[None]
    return keys, anchor_new.reshape(anchor.shape), momentum_new.reshape(momentum.shape)


def solution(mesh):
    return jax.shard_map(
        per_device,
        mesh=mesh,
        in_specs=(
            P("replica", "fsdp", None),
            P("replica", "fsdp", "tensor"),
            P("fsdp", "tensor", "replica", None),
            P("fsdp", "tensor", "replica", None),
        ),
        out_specs=(
            P("replica", "fsdp", "tensor"),
            P("fsdp", "tensor", "replica", None),
            P("fsdp", "tensor", "replica", None),
        ),
        check_vma=False,
    )
```

```python
import functools

import jax
import jax.numpy as jnp
from jax import lax
from jax.experimental import pallas as pl
from jax.experimental.pallas import tpu as pltpu
from jax.sharding import PartitionSpec as P

outer_rate = 0.7
momentum_keep = 0.9

AXES = ("replica", "fsdp", "tensor")
STEPS = (1, -1, 2)
VMEM_LIMIT = 20 * 1024 * 1024


def pairs(move):
    out = []
    for x in range(4):
        for y in range(2):
            for z in range(8):
                for c in range(2):
                    for t in range(2):
                        to_x, to_y, to_z, to_c = move(x, y, z, c)
                        source = (x * 32 + y * 16 + z * 2 + c) * 2 + t
                        target = ((to_x % 4) * 32 + (to_y % 2) * 16 + (to_z % 8) * 2 + to_c % 2) * 2 + t
                        out.append((source, target))
    return out


def send(value, move):
    return lax.ppermute(value, AXES, pairs(move))


def along_x(step):
    return lambda x, y, z, c: (x + step, y, z, c)


def early(step):
    def move(x, y, z, c):
        along_z = step if step != 2 or z % 2 == 0 else -step
        return (x + step, y, z, c) if c == 1 else (x, y, z + along_z, c)

    return move


def late(step):
    return lambda x, y, z, c: (x, y, z + step, c) if c == 1 else (x + step, y, z, c)


def position():
    index = lax.axis_index("fsdp")
    return lax.axis_index("replica"), index // 16, (index // 2) % 8, index % 2


def wrap(value):
    return lax.rem(value + 4, 4)


def call(kernel, out_shape, *, flops=0, size=1, scratch=(), in_specs=None, limit=VMEM_LIMIT):
    specs = {} if in_specs is None else {"in_specs": in_specs}
    return pl.pallas_call(
        kernel,
        out_shape=out_shape,
        **specs,
        scratch_shapes=list(scratch),
        compiler_params=pltpu.CompilerParams(vmem_limit_bytes=limit),
        cost_estimate=pl.CostEstimate(flops=flops, bytes_accessed=size, transcendentals=0),
    )


def split_kernel(grad, *outs):
    x, _, _, _ = position()
    for step, out in zip((0,) + STEPS, outs):
        first = pl.multiple_of(wrap(x + step) * 128, 128)
        out[...] = grad[:, pl.ds(first, 128)]


def prepare_kernel(anchor, momentum, anchor_out, kept_out):
    anchor_out[...] = anchor[...]
    kept_out[...] = momentum_keep * momentum[...]


def step_of(own, one, two, three, anchor, kept):
    total = own[...].astype(jnp.float32) + one[...].astype(jnp.float32)
    total = total + (two[...].astype(jnp.float32) + three[...].astype(jnp.float32))
    delta = total * 0.25
    momentum_new = kept[...] + delta
    return anchor[...] - outer_rate * (delta + momentum_keep * momentum_new), momentum_new


def weights_kernel(own, one, two, three, anchor, kept, weights):
    weights[...] = step_of(own, one, two, three, anchor, kept)[0].astype(jnp.bfloat16)


def state_kernel(own, one, two, three, anchor, kept, anchor_new, momentum_new):
    anchor_new[...], momentum_new[...] = step_of(own, one, two, three, anchor, kept)


def join_far_kernel(own, other, out):
    _, _, z, _ = position()
    far = z // 4
    out[far] = own[...]
    out[1 - far] = other[...]


def join_y_kernel(own, other, out):
    _, y, _, _ = position()
    out[pl.ds(y * 2, 2)] = own[...]
    out[pl.ds((1 - y) * 2, 2)] = other[...]


def join_four_kernel(own, one, two, three, low, high):
    x, _, z, c = position()
    here = jnp.where(c == 1, x, z % 4)
    for step, piece in zip((0,) + STEPS, (own, one, two, three)):
        place = wrap(here - step)
        row = lax.rem(place, 2) * 4

        @pl.when(place < 2)
        def _():
            low[pl.ds(row, 4)] = piece[...]

        @pl.when(place >= 2)
        def _():
            high[pl.ds(row, 4)] = piece[...]


def pack_kernel(tokens, out, sems):
    _, _, _, c = position()
    copies = []
    for near in range(4):
        for pair in range(4):
            row = (pair // 2) * 16 + ((pair % 2) * 4 + near) * 2
            source = pl.multiple_of((row + c) * 256, 256)
            copies.append(
                pltpu.make_async_copy(
                    tokens.at[:, pl.ds(source, 256)],
                    out.at[:, pl.ds((near * 4 + pair) * 256, 256)],
                    sems.at[len(copies)],
                )
            )
    for copy in copies:
        copy.start()
    for copy in copies:
        copy.wait()


def pack(tokens, space, limit):
    return call(
        pack_kernel,
        jax.ShapeDtypeStruct((512, 4096), jnp.bfloat16),
        size=2**23,
        scratch=(pltpu.SemaphoreType.DMA((16,)),),
        in_specs=[pl.BlockSpec(memory_space=space)],
        limit=limit,
    )(tokens)


def product_kernel(steps, sides, has_start, *refs):
    packed, refs = refs[: len(sides)], refs[len(sides) :]
    count = len(steps)
    lows, highs = refs[:count], refs[count : 2 * count]
    starts = refs[2 * count : 2 * count + len(sides)] if has_start else (None,) * len(sides)
    outs = refs[len(refs) - len(sides) :]
    x, _, z, c = position()

    @pl.when(c == 1)
    def _():
        for rows, start, out in zip(packed, starts, outs):
            for half, pieces in enumerate((lows, highs)):
                columns = pl.ds(half * 256, 256)
                total = start[:, columns] if has_start else None
                for step, piece in zip(steps, pieces):
                    near = pl.multiple_of(wrap(z % 4 - step) * 1024, 1024)
                    block = jnp.concatenate([piece[pl.ds(q * 4, 4)].reshape(1024, 128) for q in range(2)], axis=1)
                    term = jnp.dot(rows[:, pl.ds(near, 1024)], block, preferred_element_type=jnp.float32)
                    total = term if total is None else total + term
                out[:, columns] = total.astype(out.dtype)

    @pl.when(c == 0)
    def _():
        for rows, start, out in zip(packed, starts, outs):
            total = None
            for half, pieces in enumerate((lows, highs)):
                block = jnp.concatenate([piece[...].reshape(2048, 128) for piece in pieces], axis=1)
                term = jnp.dot(rows[:, pl.ds(half * 2048, 2048)], block, preferred_element_type=jnp.float32)
                total = term if total is None else total + term
            if has_start:
                out[...] = start[...].astype(out.dtype)
            for k, step in enumerate(steps):
                column = pl.multiple_of(wrap(x - step) * 128, 128)
                out[:, pl.ds(column, 128)] = total[:, k * 128 : (k + 1) * 128].astype(out.dtype)


def product(packed, steps, lows, highs, sides, starts=(), dtype=jnp.float32):
    count = len(steps) * len(sides)
    return call(
        functools.partial(product_kernel, steps, sides, bool(starts)),
        (jax.ShapeDtypeStruct((512, 512), dtype),) * len(sides),
        flops=2 * count * 512 * 1024 * 512,
        size=count * 2**20,
    )(*[packed[side] for side in sides], *lows, *highs, *starts)


def per_device(tokens, pseudo_grad, anchor, momentum):
    def blocks(count):
        return jax.ShapeDtypeStruct((count, 256, 128), jnp.bfloat16)

    block = jax.ShapeDtypeStruct((256, 128), jnp.bfloat16)
    state = jax.ShapeDtypeStruct((256, 128), jnp.float32)
    own_tokens = tokens[0]
    grads = call(split_kernel, (block,) * 4, size=2**19)(pseudo_grad[0])
    arrived = [send(grads[k + 1], along_x(step)) for k, step in enumerate(STEPS)]
    other_tokens = send(own_tokens, lambda x, y, z, c: (x, y, z, c + 1))
    prepared = call(prepare_kernel, (state, state), size=2**19)(anchor.reshape(256, 128), momentum.reshape(256, 128))
    (weights,) = call(weights_kernel, (block,), size=2**19)(grads[0], *arrived, *prepared)
    anchor_new, momentum_new = call(state_kernel, (state, state), size=2**20)(grads[0], *arrived, *prepared)
    by_far = send(weights, lambda x, y, z, c: (x, y, z + 4, c))
    (two,) = call(join_far_kernel, (blocks(2),), size=2**18)(weights, by_far)
    by_y = send(two, lambda x, y, z, c: (x, y + 1, z, c))
    packed_own = pack(own_tokens, pltpu.HBM, 44 * 1024 * 1024)
    two, packed_own = lax.optimization_barrier((two, packed_own))
    (four,) = call(join_y_kernel, (blocks(4),), size=2**19)(two, by_y)
    fours = [send(four, early(step)) for step in STEPS]
    packed_other = pack(other_tokens, pltpu.VMEM, VMEM_LIMIT)
    four, packed_other = lax.optimization_barrier((four, packed_other))
    packed = (packed_own, packed_other)
    low, high = call(join_four_kernel, (blocks(8), blocks(8)), size=2**21)(four, *fours)
    low_up, high_down = send(low, late(1)), send(high, late(-1))
    high_up, low_down = send(high, late(1)), send(low, late(-1))
    starts = product(packed, (0,), (low,), (high,), (0, 1))
    low_up, high_down, *starts = lax.optimization_barrier((low_up, high_down, *starts))
    low_two, high_two = send(low_up, late(1)), send(high_down, late(-1))
    starts = product(packed, (1, -1), (low_up, low_down), (high_up, high_down), (0, 1), starts)
    (away,) = product(packed, (2,), (low_two,), (high_two,), (1,), starts[1:], jnp.bfloat16)
    returned = send(away, lambda x, y, z, c: (x, y, z, c + 1))
    (here,) = product(packed, (2,), (low_two,), (high_two,), (0,), starts[:1])
    keys = (here + returned.astype(jnp.float32)).astype(jnp.bfloat16)[None]
    return keys, anchor_new.reshape(anchor.shape), momentum_new.reshape(momentum.shape)


def solution(mesh):
    return jax.shard_map(
        per_device,
        mesh=mesh,
        in_specs=(
            P("replica", "fsdp", None),
            P("replica", "fsdp", "tensor"),
            P("fsdp", "tensor", "replica", None),
            P("fsdp", "tensor", "replica", None),
        ),
        out_specs=(
            P("replica", "fsdp", "tensor"),
            P("fsdp", "tensor", "replica", None),
            P("fsdp", "tensor", "replica", None),
        ),
        check_vma=False,
    )
```

```python
import functools

import jax
import jax.numpy as jnp
from jax import lax
from jax.experimental import pallas as pl
from jax.experimental.pallas import tpu as pltpu
from jax.sharding import PartitionSpec as P

outer_rate = 0.7
momentum_keep = 0.9

AXES = ("replica", "fsdp", "tensor")
STEPS = (1, -1, 2)
VMEM_LIMIT = 20 * 1024 * 1024


def pairs(move):
    out = []
    for x in range(4):
        for y in range(2):
            for z in range(8):
                for c in range(2):
                    for t in range(2):
                        to_x, to_y, to_z, to_c = move(x, y, z, c)
                        source = (x * 32 + y * 16 + z * 2 + c) * 2 + t
                        target = ((to_x % 4) * 32 + (to_y % 2) * 16 + (to_z % 8) * 2 + to_c % 2) * 2 + t
                        out.append((source, target))
    return out


def send(value, move):
    return lax.ppermute(value, AXES, pairs(move))


def along_x(step):
    return lambda x, y, z, c: (x + step, y, z, c)


def early(step):
    def move(x, y, z, c):
        along_z = step if step != 2 or z % 2 == 0 else -step
        return (x + step, y, z, c) if c == 1 else (x, y, z + along_z, c)

    return move


def late(step):
    return lambda x, y, z, c: (x, y, z + step, c) if c == 1 else (x + step, y, z, c)


def position():
    index = lax.axis_index("fsdp")
    return lax.axis_index("replica"), index // 16, (index // 2) % 8, index % 2


def wrap(value):
    return lax.rem(value + 4, 4)


def call(kernel, out_shape, *, flops=0, size=1, scratch=(), in_specs=None, limit=VMEM_LIMIT):
    specs = {} if in_specs is None else {"in_specs": in_specs}
    return pl.pallas_call(
        kernel,
        out_shape=out_shape,
        **specs,
        scratch_shapes=list(scratch),
        compiler_params=pltpu.CompilerParams(vmem_limit_bytes=limit),
        cost_estimate=pl.CostEstimate(flops=flops, bytes_accessed=size, transcendentals=0),
    )


def split_kernel(grad, *outs):
    x, _, _, _ = position()
    for step, out in zip((0,) + STEPS, outs):
        first = pl.multiple_of(wrap(x + step) * 128, 128)
        out[...] = grad[:, pl.ds(first, 128)]


def prepare_kernel(anchor, momentum, anchor_out, kept_out):
    anchor_out[...] = anchor[...]
    kept_out[...] = momentum_keep * momentum[...]


def step_of(own, one, two, three, anchor, kept):
    total = own[...].astype(jnp.float32) + one[...].astype(jnp.float32)
    total = total + (two[...].astype(jnp.float32) + three[...].astype(jnp.float32))
    delta = total * 0.25
    momentum_new = kept[...] + delta
    return anchor[...] - outer_rate * (delta + momentum_keep * momentum_new), momentum_new


def weights_kernel(own, one, two, three, anchor, kept, weights):
    weights[...] = step_of(own, one, two, three, anchor, kept)[0].astype(jnp.bfloat16)


def state_kernel(own, one, two, three, anchor, kept, anchor_new, momentum_new):
    anchor_new[...], momentum_new[...] = step_of(own, one, two, three, anchor, kept)


def join_pair_kernel(own, other, out):
    _, y, z, c = position()
    here = jnp.where(c == 0, z // 4, y)
    out[here] = own[...]
    out[1 - here] = other[...]


def join_pairs_kernel(own, other, out):
    _, y, z, c = position()
    far = z // 4

    @pl.when(c == 0)
    def _():
        out[pl.ds(y * 2, 2)] = own[...]
        out[pl.ds((1 - y) * 2, 2)] = other[...]

    @pl.when(c == 1)
    def _():
        for k in range(2):
            out[k * 2 + far] = own[k]
            out[k * 2 + 1 - far] = other[k]


def join_four_kernel(own, one, two, three, low, high):
    x, _, z, c = position()
    here = jnp.where(c == 1, x, z % 4)
    for step, piece in zip((0,) + STEPS, (own, one, two, three)):
        place = wrap(here - step)
        row = lax.rem(place, 2) * 4

        @pl.when(place < 2)
        def _():
            low[pl.ds(row, 4)] = piece[...]

        @pl.when(place >= 2)
        def _():
            high[pl.ds(row, 4)] = piece[...]


def pack_kernel(tokens, out, sems):
    _, _, _, c = position()
    copies = []
    for near in range(4):
        for pair in range(4):
            row = (pair // 2) * 16 + ((pair % 2) * 4 + near) * 2
            source = pl.multiple_of((row + c) * 256, 256)
            copies.append(
                pltpu.make_async_copy(
                    tokens.at[:, pl.ds(source, 256)],
                    out.at[:, pl.ds((near * 4 + pair) * 256, 256)],
                    sems.at[len(copies)],
                )
            )
    for copy in copies:
        copy.start()
    for copy in copies:
        copy.wait()


def pack(tokens, space, limit):
    return call(
        pack_kernel,
        jax.ShapeDtypeStruct((512, 4096), jnp.bfloat16),
        size=2**23,
        scratch=(pltpu.SemaphoreType.DMA((16,)),),
        in_specs=[pl.BlockSpec(memory_space=space)],
        limit=limit,
    )(tokens)


def product_kernel(steps, sides, has_start, *refs):
    packed, refs = refs[: len(sides)], refs[len(sides) :]
    count = len(steps)
    lows, highs = refs[:count], refs[count : 2 * count]
    starts = refs[2 * count : 2 * count + len(sides)] if has_start else (None,) * len(sides)
    outs = refs[len(refs) - len(sides) :]
    x, _, z, c = position()

    @pl.when(c == 1)
    def _():
        for rows, start, out in zip(packed, starts, outs):
            for half, pieces in enumerate((lows, highs)):
                columns = pl.ds(half * 256, 256)
                total = start[:, columns] if has_start else None
                for step, piece in zip(steps, pieces):
                    near = pl.multiple_of(wrap(z % 4 - step) * 1024, 1024)
                    block = jnp.concatenate([piece[pl.ds(q * 4, 4)].reshape(1024, 128) for q in range(2)], axis=1)
                    term = jnp.dot(rows[:, pl.ds(near, 1024)], block, preferred_element_type=jnp.float32)
                    total = term if total is None else total + term
                out[:, columns] = total.astype(out.dtype)

    @pl.when(c == 0)
    def _():
        for rows, start, out in zip(packed, starts, outs):
            total = None
            for half, pieces in enumerate((lows, highs)):
                block = jnp.concatenate([piece[...].reshape(2048, 128) for piece in pieces], axis=1)
                term = jnp.dot(rows[:, pl.ds(half * 2048, 2048)], block, preferred_element_type=jnp.float32)
                total = term if total is None else total + term
            if has_start:
                out[...] = start[...].astype(out.dtype)
            for k, step in enumerate(steps):
                column = pl.multiple_of(wrap(x - step) * 128, 128)
                out[:, pl.ds(column, 128)] = total[:, k * 128 : (k + 1) * 128].astype(out.dtype)


def product(packed, steps, lows, highs, sides, starts=(), dtype=jnp.float32):
    count = len(steps) * len(sides)
    return call(
        functools.partial(product_kernel, steps, sides, bool(starts)),
        (jax.ShapeDtypeStruct((512, 512), dtype),) * len(sides),
        flops=2 * count * 512 * 1024 * 512,
        size=count * 2**20,
    )(*[packed[side] for side in sides], *lows, *highs, *starts)


def per_device(tokens, pseudo_grad, anchor, momentum):
    def blocks(count):
        return jax.ShapeDtypeStruct((count, 256, 128), jnp.bfloat16)

    block = jax.ShapeDtypeStruct((256, 128), jnp.bfloat16)
    state = jax.ShapeDtypeStruct((256, 128), jnp.float32)
    own_tokens = tokens[0]
    grads = call(split_kernel, (block,) * 4, size=2**19)(pseudo_grad[0])
    parts = dict(zip(STEPS, grads[1:]))
    arrived = [send(parts[step], along_x(step)) for step in (1, 2, -1)]
    other_tokens = send(own_tokens, lambda x, y, z, c: (x, y, z, c + 1))
    prepared = call(prepare_kernel, (state, state), size=2**19)(anchor.reshape(256, 128), momentum.reshape(256, 128))
    (weights,) = call(weights_kernel, (block,), size=2**19)(grads[0], *arrived, *prepared)
    anchor_new, momentum_new = call(state_kernel, (state, state), size=2**20)(grads[0], *arrived, *prepared)
    def over_far(x, y, z, c):
        return x, y, z + 4, c

    def over_y(x, y, z, c):
        return x, y + 1, z, c

    pair = send(weights, lambda x, y, z, c: over_far(x, y, z, c) if c == 0 else over_y(x, y, z, c))
    (two,) = call(join_pair_kernel, (blocks(2),), size=2**18)(weights, pair)
    pair = send(two, lambda x, y, z, c: over_y(x, y, z, c) if c == 0 else over_far(x, y, z, c))
    packed_own = pack(own_tokens, pltpu.HBM, 44 * 1024 * 1024)
    two, packed_own = lax.optimization_barrier((two, packed_own))
    (four,) = call(join_pairs_kernel, (blocks(4),), size=2**19)(two, pair)
    fours = [send(four, early(step)) for step in STEPS]
    packed_other = pack(other_tokens, pltpu.VMEM, VMEM_LIMIT)
    four, packed_other = lax.optimization_barrier((four, packed_other))
    packed = (packed_own, packed_other)
    low, high = call(join_four_kernel, (blocks(8), blocks(8)), size=2**21)(four, *fours)
    low_up, high_down = send(low, late(1)), send(high, late(-1))
    high_up, low_down = send(high, late(1)), send(low, late(-1))
    starts = product(packed, (0,), (low,), (high,), (0, 1))
    low_up, high_down, *starts = lax.optimization_barrier((low_up, high_down, *starts))
    low_two, high_two = send(low_up, late(1)), send(high_down, late(-1))
    starts = product(packed, (1, -1), (low_up, low_down), (high_up, high_down), (0, 1), starts)
    (away,) = product(packed, (2,), (low_two,), (high_two,), (1,), starts[1:], jnp.bfloat16)
    returned = send(away, lambda x, y, z, c: (x, y, z, c + 1))
    (here,) = product(packed, (2,), (low_two,), (high_two,), (0,), starts[:1])
    keys = (here + returned.astype(jnp.float32)).astype(jnp.bfloat16)[None]
    return keys, anchor_new.reshape(anchor.shape), momentum_new.reshape(momentum.shape)


def solution(mesh):
    return jax.shard_map(
        per_device,
        mesh=mesh,
        in_specs=(
            P("replica", "fsdp", None),
            P("replica", "fsdp", "tensor"),
            P("fsdp", "tensor", "replica", None),
            P("fsdp", "tensor", "replica", None),
        ),
        out_specs=(
            P("replica", "fsdp", "tensor"),
            P("fsdp", "tensor", "replica", None),
            P("fsdp", "tensor", "replica", None),
        ),
        check_vma=False,
    )
```
